512 devices in a mesh: group: 16 (over x, z_lo), dp: 32 (over y, z_hi, core).
Axes of the slice: x: 4, y: 4, z: 16 (z_hi: 4, z_lo: 4; z = z_hi * 4 + z_lo), core: 2. Of those that a mesh axis runs over, the one named last changes fastest.
Arguments:
- embeddings: float32 [131072, 512], P(('group', 'dp')), may hold values from -8 to 8
- partner: int32 [131072], replicated, may hold values from 0 to 131071, as said below
Outputs:
- gradient: float32 [131072, 512], P(('group', 'dp'))
- loss: float32 [], replicated
The draws below stay inside these ranges and needn't reach their ends.
Inputs may be any that keep to these rules, and one draw needn't show every extreme that they name: partner[partner[i]] == i and partner[i] != i, and partner[i] lies in the same batch as i: the rows of each batch form 4096/2 pairs of views, drawn at random.
All inputs are finite; a program needn't handle non-finite values.
Results may differ from the reference program's by a relative error of at most 0.00095.
The reference program's roundings to bfloat16 on the way (of `packed` and `weights`) count: a program that leaves them out, or rounds other values in their place, can miss the bound.
Values may be sent and summed in bfloat16 or wider, within the bound.
No kernel may reach another device: no remote copies, remote signals or barrier semaphores. Data moves between devices by JAX's collectives and lax.ppermute only.
A program may use at most 64 MiB of HBM per device.

```python
import math
import jax
import jax.numpy as jnp
from jax import lax

E = 512
ROWS_DEV = 256
ROWS = 131072
N_GROUP = 16
N_DP = 32


def pair_orders(key):
    key = jax.random.fold_in(key, 5)
    span = ROWS_DEV * N_GROUP
    keys = jax.random.split(key, N_DP)
    return jax.vmap(lambda single: jax.random.permutation(single, span))(keys).astype(jnp.int32)


def draw_partner(key, part):
    orders = pair_orders(key)
    span = ROWS_DEV * N_GROUP
    first = orders[:, 0::2]
    second = orders[:, 1::2]
    batch_ids = jnp.arange(N_DP, dtype=jnp.int32)[:, None]
    local = jnp.zeros((N_DP, span), jnp.int32)
    local = local.at[batch_ids, first].set(second).at[batch_ids, second].set(first)
    global_ids = (local // ROWS_DEV * N_DP + batch_ids) * ROWS_DEV + local % ROWS_DEV
    paired = global_ids.reshape(N_DP, N_GROUP, ROWS_DEV).transpose(1, 0, 2).reshape(ROWS)
    return paired.astype(jnp.int32)


def draw_embeddings(key, part):
    orders = pair_orders(key)
    key = jax.random.fold_in(key, 9)
    span = ROWS_DEV * N_GROUP
    half = span // 2
    centre_count = max(2, span // 64)
    keys = jax.random.split(key, 5)
    batch_ids = jnp.arange(N_DP, dtype=jnp.int32)[:, None]
    positions = jnp.broadcast_to(jnp.arange(span, dtype=jnp.int32)[None, :] // 2, (N_DP, span))
    clip_of = jnp.zeros((N_DP, span), jnp.int32).at[batch_ids, orders].set(positions)
    cluster = jax.random.randint(keys[0], (N_DP, half), 0, centre_count).astype(jnp.int32)
    scale = float(E) ** (-0.5)
    centres = jax.random.truncated_normal(keys[1], -3.0, 3.0, (N_DP, centre_count, E), jnp.float32) * scale
    clip_noise = jax.random.truncated_normal(keys[2], -3.0, 3.0, (N_DP, half, E), jnp.float32) * scale
    view_noise = jax.random.truncated_normal(keys[3], -3.0, 3.0, (N_DP, span, E), jnp.float32) * scale
    strength = jnp.exp(jax.random.uniform(keys[4], (N_DP, half), jnp.float32, math.log(0.2), math.log(2.5)))
    clip_vectors = strength[:, :, None] * centres[batch_ids, cluster] + clip_noise
    views = clip_vectors[batch_ids, clip_of] + 0.8 * view_noise
    whole = views.reshape(N_DP, N_GROUP, ROWS_DEV, E).transpose(1, 0, 2, 3).reshape(ROWS, E)
    return whole.astype(jnp.float32)


def setup_inputs(seed: int = 0) -> dict:
    key_list = jax.random.split(jax.random.key(seed), 3)
    return {
        "embeddings": draw_embeddings(jax.random.fold_in(key_list[2], 71), 0),
        "partner": draw_partner(jax.random.fold_in(key_list[2], 71), 0),
    }


TAU = 0.1

def reference(embeddings, partner):
    span = ROWS_DEV * N_GROUP
    lengths = jnp.sqrt(lax.optimization_barrier(jnp.sum(embeddings * embeddings, axis=1, keepdims=True)) + 1e-06)
    unit = embeddings / lengths
    packed = unit.astype(jnp.bfloat16)
    batches = packed.reshape(N_GROUP, N_DP, ROWS_DEV, E).transpose(1, 0, 2, 3).reshape(N_DP, span, E)
    pairs = partner.reshape(N_GROUP, N_DP, ROWS_DEV).transpose(1, 0, 2).reshape(N_DP, span)
    pairs = (pairs // (N_DP * ROWS_DEV) * ROWS_DEV + pairs % ROWS_DEV).astype(jnp.int32)
    places = jnp.arange(span, dtype=jnp.int32)

    def visit(loss_total, item):
        block_units, local_pair = item
        scores = jnp.dot(block_units, block_units.T, preferred_element_type=jnp.float32) / TAU
        on_diagonal = places[:, None] == places[None, :]
        weights_exp = jnp.where(on_diagonal, jnp.float32(0.0), jnp.exp(scores - 1.0 / TAU))
        is_partner = places[None, :] == local_pair[:, None]
        totals = lax.optimization_barrier(jnp.sum(weights_exp, axis=1))
        positive = lax.optimization_barrier(jnp.sum(jnp.where(is_partner, scores, jnp.float32(0.0)), axis=1))
        loss_rows = jnp.log(totals) + 1.0 / TAU - positive
        weights = (weights_exp / totals[:, None] - is_partner.astype(jnp.float32)).astype(jnp.bfloat16)
        row_part = jnp.dot(weights, block_units, preferred_element_type=jnp.float32)
        col_part = jnp.dot(weights.T, block_units, preferred_element_type=jnp.float32)
        return (loss_total + jnp.sum(loss_rows), row_part + col_part)
    loss_total, parts = lax.scan(visit, jnp.zeros((), jnp.float32), (batches, pairs))
    unit_grad = parts.reshape(N_DP, N_GROUP, ROWS_DEV, E).transpose(1, 0, 2, 3).reshape(ROWS, E) / TAU
    gradient = (unit_grad - unit * lax.optimization_barrier(jnp.sum(unit * unit_grad, axis=1, keepdims=True))) / lengths
    return (gradient, loss_total / ROWS)
```

```python
import functools

import jax
import jax.numpy as jnp
from jax import lax
from jax.experimental import pallas as pl
from jax.experimental.pallas import tpu as pltpu
from jax.sharding import PartitionSpec as P

TAU = 0.1
LOG2E = 1.4426950408889634
SCALE = LOG2E / TAU
X = 4
Z = 4
B = 256
E = 512
SLOTS = X * Z
ORDER = [
    (0, 0), (0, 1), (0, 2), (0, 3),
    (1, 0), (1, 1), (3, 0), (3, 1),
    (1, 2), (1, 3), (3, 2), (3, 3),
    (2, 0), (2, 1),
    (2, 2), (2, 3),
]
STAGES = (4, 8, 12, 14, 16)
CHUNK = 1024
MIB = 1024 * 1024
VMEM = pl.BlockSpec(memory_space=pltpu.VMEM)
HBM = pl.BlockSpec(memory_space=pltpu.HBM)


def nt_dot(a, b):
    return lax.dot_general(a, b, (((1,), (1,)), ((), ())), preferred_element_type=jnp.float32)


def column(row):
    return jnp.broadcast_to(row, (128, B)).T


def pack_kernel(emb_ref, packed_ref):
    emb = emb_ref[...]
    lengths = jnp.sqrt(jnp.sum(emb * emb, axis=1, keepdims=True) + 1e-06)
    packed_ref[...] = (emb / lengths).astype(jnp.bfloat16)


def pack(embeddings):
    return pl.pallas_call(
        pack_kernel,
        out_shape=jax.ShapeDtypeStruct((B, E), jnp.bfloat16),
        in_specs=[VMEM],
        out_specs=VMEM,
        compiler_params=pltpu.CompilerParams(vmem_limit_bytes=4 * MIB),
    )(embeddings)


def owners():
    group_pos = lax.axis_index("group")
    own_x, own_z = lax.div(group_pos, Z), lax.rem(group_pos, Z)
    way = 1 - 2 * lax.rem(lax.axis_index("dp"), 2)
    return [((own_x - way * back_x) & (X - 1)) * Z + (own_z ^ mask) for back_x, mask in ORDER]


def place_kernel(dp_count, partner_ref, place_ref, own_ref, near, sem):
    group_pos = lax.axis_index("group")
    own_x, own_z = lax.div(group_pos, Z), lax.rem(group_pos, Z)
    lines = B // 128
    starts = [(owner * dp_count + lax.axis_index("dp")) * lines for owner in owners()]
    bases = [pl.multiple_of(lax.div(start, 8) * 8, 8) for start in starts]
    copies = [
        pltpu.make_async_copy(partner_ref.at[pl.ds(base, 8), :], near.at[k], sem.at[k])
        for k, base in enumerate(bases)
    ]
    for copy in copies:
        copy.start()
    for copy in copies:
        copy.wait()
    for s in range(SLOTS):
        for line in range(lines):
            row = near[s, pl.ds(starts[s] - bases[s] + line, 1), :]
            place_ref[s : s + 1, line * 128 : (line + 1) * 128] = row
    partner = place_ref[...]
    far = partner // (dp_count * B)
    way = 1 - 2 * lax.rem(lax.axis_index("dp"), 2)
    back = ((way * (own_x - far // Z)) & (X - 1)) * Z + ((far & (Z - 1)) ^ own_z)
    slot = jnp.zeros_like(back)
    for k, (back_x, mask) in enumerate(ORDER):
        slot = jnp.where(back == back_x * Z + mask, k, slot)
    place = slot * B + (partner & (B - 1))
    place_ref[...] = place
    own_ref[...] = column(place[0:1, :])


def places(partner, dp_count):
    return pl.pallas_call(
        functools.partial(place_kernel, dp_count),
        out_shape=(
            jax.ShapeDtypeStruct((SLOTS, B), jnp.int32),
            jax.ShapeDtypeStruct((B, 128), jnp.int32),
        ),
        in_specs=[HBM],
        out_specs=(VMEM, VMEM),
        scratch_shapes=[pltpu.VMEM((SLOTS, 8, 128), jnp.int32), pltpu.SemaphoreType.DMA((SLOTS,))],
        compiler_params=pltpu.CompilerParams(vmem_limit_bytes=4 * MIB),
    )(pltpu.with_memory_space_constraint(partner.reshape(-1, 128), pltpu.HBM))


def split_blocks(pieces):
    return [(piece, row) for piece in pieces for row in range(0, piece.shape[0], B)]


def sums_kernel(first, last, n_pieces, n_old, *refs):
    pieces = refs[:n_pieces]
    place_ref = refs[n_pieces]
    sums_in = refs[n_pieces + 1] if first > 0 else None
    sums_out, units_out, *part_out, sem = refs[n_pieces + (2 if first > 0 else 1) :]
    copies, done = [], 0
    for k, piece in enumerate(pieces[n_old:]):
        rows = piece.shape[0]
        copies.append(pltpu.make_async_copy(piece, units_out.at[pl.ds(done, rows), :], sem.at[k]))
        done += rows
    for copy in copies:
        copy.start()
    blocks = [piece[row : row + B, :] for piece, row in split_blocks(pieces)]
    rows = lax.broadcasted_iota(jnp.int32, (B, B), 0)
    lanes = lax.broadcasted_iota(jnp.int32, (B, B), 1)
    place = place_ref[...]

    def fold(value):
        return jnp.sum(value.reshape(B // 8, 8, B), axis=0)

    sums = [jnp.zeros((8, B), jnp.float32)] * last
    hits = jnp.zeros((8, B), jnp.float32)
    row_sums = {}
    for a in range(first, last):
        total = jnp.zeros((B, 128), jnp.float32)
        for c in [*range(first), *range(a, last)]:
            raw = nt_dot(blocks[a], blocks[c])
            e = jnp.exp2(raw * SCALE)
            if c == a:
                e = jnp.where(rows == lanes, 0.0, e)
            total = total + (e[:, :128] + e[:, 128:])
            found = fold(jnp.where(rows == place[c : c + 1, :] - a * B, raw, 0.0))
            if c != a:
                sums[c] = sums[c] + fold(e)
                found = 2.0 * found
            hits = hits + found
        row_sums[a] = jnp.sum(total.T, axis=0, keepdims=True)
    for s in range(last):
        total = jnp.sum(sums[s], axis=0, keepdims=True)
        total = total + (sums_in[s : s + 1, :] if s < first else row_sums[s])
        sums_out[s : s + 1, :] = total
    if last < SLOTS:
        sums_out[last:SLOTS, :] = jnp.zeros((SLOTS - last, B), jnp.float32)
    if first > 0:
        hits = hits + sums_in[SLOTS:, :]
    sums_out[SLOTS:, :] = hits
    if last == SLOTS:
        logs = jnp.log(sums_out[:SLOTS, :])
        part = jnp.sum(logs, axis=0, keepdims=True) - jnp.sum(hits, axis=0, keepdims=True) * (1.0 / TAU)
        part = part[:, :128] + part[:, 128:]
        part_out[0][...] = jnp.broadcast_to(part[None], part_out[0].shape)
    for copy in copies:
        copy.wait()


def sums(first, last, old, new, place, state, dp_count):
    pairs = (last - first) * (last + first + 1) // 2
    operands = list(old) + list(new) + [place] + list(state)
    is_last = last == SLOTS
    return pl.pallas_call(
        functools.partial(sums_kernel, first, last, len(old) + len(new), len(old)),
        out_shape=(
            jax.ShapeDtypeStruct((SLOTS + 8, B), jnp.float32),
            pltpu.HBM(((last - first) * B, E), jnp.bfloat16),
        )
        + ((jax.ShapeDtypeStruct((dp_count, 1, 128), jnp.float32),) if is_last else ()),
        in_specs=[VMEM] * len(operands),
        out_specs=(VMEM, HBM) + ((VMEM,) if is_last else ()),
        scratch_shapes=[pltpu.SemaphoreType.DMA((len(new),))],
        compiler_params=pltpu.CompilerParams(vmem_limit_bytes=12 * MIB),
        cost_estimate=pl.CostEstimate(
            flops=pairs * 2 * B * B * E, bytes_accessed=last * B * E * 2, transcendentals=pairs * B * B
        ),
    )(*operands)


def grad_kernel(*refs):
    unit_refs = refs[: len(STAGES)]
    place_ref, totals_ref, emb_ref, grad_ref, units, sem = refs[len(STAGES) :]
    copies = []
    for k, (ref, row) in enumerate(split_blocks(unit_refs)):
        target = units.at[pl.ds(k * B, B), :]
        copies.append(pltpu.make_async_copy(ref.at[pl.ds(row, B), :], target, sem.at[k]))
    for copy in copies:
        copy.start()
    inverse = 1.0 / totals_ref[:SLOTS, :]
    row_inv = column(inverse[0:1, :])
    row_inv = jnp.concatenate([row_inv, row_inv], axis=1)
    place = jnp.concatenate([place_ref[...], place_ref[...]], axis=1)
    rows = lax.broadcasted_iota(jnp.int32, (B, B), 0)
    lanes = lax.broadcasted_iota(jnp.int32, (B, B), 1)
    emb = emb_ref[...]
    lengths = jnp.sqrt(jnp.sum(emb * emb, axis=1, keepdims=True) + 1e-06)
    unit = emb / lengths
    unit_grad = None
    for start in range(0, SLOTS * B, CHUNK):
        for copy in copies[start // B : (start + CHUNK) // B]:
            copy.wait()
        cols = units[start : start + CHUNK, :]
        raw = nt_dot(units[0:B, :], cols)
        row_w, col_w = [], []
        for k in range(CHUNK // B):
            b = start // B + k
            e = jnp.exp2(raw[:, k * B : (k + 1) * B] * SCALE)
            if b == 0:
                e = jnp.where(rows == lanes, 0.0, e)
            ind = jnp.where(lanes + b * B == place, 1.0, 0.0)
            row_w.append((e * row_inv - ind).astype(jnp.bfloat16))
            col_w.append((e * inverse[b : b + 1, :] - ind).astype(jnp.bfloat16))
        both = jnp.concatenate(
            [jnp.concatenate(row_w, axis=1), jnp.concatenate(col_w, axis=1)], axis=0
        )
        both = jnp.dot(both, cols, preferred_element_type=jnp.float32)
        part = both[:B] + both[B:]
        unit_grad = part if unit_grad is None else unit_grad + part
    unit_grad = unit_grad * (1.0 / TAU)
    along = jnp.sum(unit * unit_grad, axis=1, keepdims=True)
    grad_ref[...] = (unit_grad - unit * along) / lengths


def grads(units, place, totals, embeddings):
    return pl.pallas_call(
        grad_kernel,
        out_shape=jax.ShapeDtypeStruct((B, E), jnp.float32),
        in_specs=[HBM] * len(units) + [VMEM] * 3,
        out_specs=VMEM,
        scratch_shapes=[
            pltpu.VMEM((SLOTS * B, E), jnp.bfloat16),
            pltpu.SemaphoreType.DMA((SLOTS,)),
        ],
        compiler_params=pltpu.CompilerParams(vmem_limit_bytes=16 * MIB),
        cost_estimate=pl.CostEstimate(
            flops=6 * SLOTS * B * B * E, bytes_accessed=SLOTS * B * E * 2, transcendentals=SLOTS * B * B
        ),
    )(*[pltpu.with_memory_space_constraint(part, pltpu.HBM) for part in units], place, totals, embeddings)


def shift_x(value, step):
    dp_count = lax.axis_size("dp")
    perm = []
    for x in range(X):
        for z in range(Z):
            for k in range(dp_count):
                to_x = (x + (step if k % 2 == 0 else -step)) % X
                perm.append(((x * Z + z) * dp_count + k, (to_x * Z + z) * dp_count + k))
    return lax.ppermute(value, ("group", "dp"), perm)


def swap_z(value, mask):
    perm = [(x * Z + z, x * Z + (z ^ mask)) for x in range(X) for z in range(Z)]
    return lax.ppermute(value, "group", perm)


def stack_kernel(first_ref, second_ref, both_ref):
    both_ref[:B, :] = first_ref[...]
    both_ref[B:, :] = second_ref[...]


def stack(first, second):
    return pl.pallas_call(
        stack_kernel,
        out_shape=jax.ShapeDtypeStruct((2 * B, E), jnp.bfloat16),
        in_specs=[VMEM, VMEM],
        out_specs=VMEM,
        compiler_params=pltpu.CompilerParams(vmem_limit_bytes=4 * MIB),
    )(first, second)


def on_device(embeddings, partner):
    dp_count = lax.axis_size("dp")
    group_count = lax.axis_size("group")
    packed = pack(embeddings)
    place, own_place = places(partner, dp_count)

    z1 = swap_z(packed, 1)
    z2 = swap_z(packed, 2)
    near = stack(packed, z1)
    near_1, near_3 = shift_x(near, 1), shift_x(near, 3)
    z3, place, own_place = lax.optimization_barrier((swap_z(z2, 1), place, own_place))
    far = stack(z2, z3)
    far_1, far_3 = shift_x(far, 1), shift_x(far, 3)

    old, units, state = [], [], ()

    def add(*new):
        first, last = sum(STAGES[len(units) - 1 : len(units)]), STAGES[len(units)]
        part_sums, part_units, *rest = sums(first, last, old, new, place, state, dp_count)
        units.append(part_units)
        old.extend(new)
        return (part_sums,), rest

    state, _ = add(near, far)
    state, _ = add(near_1, near_3)
    near_1, near_3, *state = lax.optimization_barrier((near_1, near_3, *state))
    near_2 = shift_x(near_1, 1)
    far_3, *state = lax.optimization_barrier((far_3, *state))
    far_2 = shift_x(far_3, 3)
    state, _ = add(far_1, far_3)
    state, _ = add(near_2)
    (totals,), (part,) = add(far_2)
    losses = lax.all_to_all(part, "dp", 0, 0)
    gradient = grads(units, own_place, totals, embeddings)
    loss = jnp.sum(losses) / (B * dp_count * group_count)
    return (gradient, loss)


def solution(mesh):
    placed = (P(("group", "dp"), None), P())
    return jax.shard_map(
        on_device,
        mesh=mesh,
        in_specs=placed,
        out_specs=(P(("group", "dp"), None), P()),
        check_vma=False,
    )
```

```python
import functools

import jax
import jax.numpy as jnp
from jax import lax
from jax.experimental import pallas as pl
from jax.experimental.pallas import tpu as pltpu
from jax.sharding import PartitionSpec as P

TAU = 0.1
LOG2E = 1.4426950408889634
SCALE = LOG2E / TAU
X = 4
Z = 4
B = 256
E = 512
SLOTS = X * Z
ORDER = [
    (0, 0), (0, 1), (0, 2), (0, 3),
    (1, 0), (1, 1), (3, 0), (3, 1),
    (1, 2), (1, 3), (3, 2), (3, 3),
    (2, 0), (2, 1),
    (2, 2), (2, 3),
]
STAGES = (4, 8, 12, 14, 16)
CHUNK = 1024
MIB = 1024 * 1024
VMEM = pl.BlockSpec(memory_space=pltpu.VMEM)
HBM = pl.BlockSpec(memory_space=pltpu.HBM)


def nt_dot(a, b):
    return lax.dot_general(a, b, (((1,), (1,)), ((), ())), preferred_element_type=jnp.float32)


def column(row):
    return jnp.broadcast_to(row, (128, B)).T


def pack_kernel(emb_ref, packed_ref):
    emb = emb_ref[...]
    lengths = jnp.sqrt(jnp.sum(emb * emb, axis=1, keepdims=True) + 1e-06)
    packed_ref[...] = (emb / lengths).astype(jnp.bfloat16)


def pack(embeddings):
    return pl.pallas_call(
        pack_kernel,
        out_shape=jax.ShapeDtypeStruct((B, E), jnp.bfloat16),
        in_specs=[VMEM],
        out_specs=VMEM,
        compiler_params=pltpu.CompilerParams(vmem_limit_bytes=4 * MIB),
    )(embeddings)


def owners():
    group_pos = lax.axis_index("group")
    own_x, own_z = lax.div(group_pos, Z), lax.rem(group_pos, Z)
    way = 1 - 2 * lax.rem(lax.axis_index("dp"), 2)
    return [((own_x - way * back_x) & (X - 1)) * Z + (own_z ^ mask) for back_x, mask in ORDER]


def place_kernel(dp_count, partner_ref, place_ref, own_ref, near, sem):
    group_pos = lax.axis_index("group")
    own_x, own_z = lax.div(group_pos, Z), lax.rem(group_pos, Z)
    lines = B // 128
    starts = [(owner * dp_count + lax.axis_index("dp")) * lines for owner in owners()]
    bases = [pl.multiple_of(lax.div(start, 8) * 8, 8) for start in starts]
    copies = [
        pltpu.make_async_copy(partner_ref.at[pl.ds(base, 8), :], near.at[k], sem.at[k])
        for k, base in enumerate(bases)
    ]
    for copy in copies:
        copy.start()
    for copy in copies:
        copy.wait()
    for s in range(SLOTS):
        for line in range(lines):
            row = near[s, pl.ds(starts[s] - bases[s] + line, 1), :]
            place_ref[s : s + 1, line * 128 : (line + 1) * 128] = row
    partner = place_ref[...]
    far = partner // (dp_count * B)
    way = 1 - 2 * lax.rem(lax.axis_index("dp"), 2)
    back = ((way * (own_x - far // Z)) & (X - 1)) * Z + ((far & (Z - 1)) ^ own_z)
    slot = jnp.zeros_like(back)
    for k, (back_x, mask) in enumerate(ORDER):
        slot = jnp.where(back == back_x * Z + mask, k, slot)
    place = slot * B + (partner & (B - 1))
    place_ref[...] = place
    own_ref[...] = column(place[0:1, :])


def places(partner, dp_count):
    return pl.pallas_call(
        functools.partial(place_kernel, dp_count),
        out_shape=(
            jax.ShapeDtypeStruct((SLOTS, B), jnp.int32),
            jax.ShapeDtypeStruct((B, 128), jnp.int32),
        ),
        in_specs=[HBM],
        out_specs=(VMEM, VMEM),
        scratch_shapes=[pltpu.VMEM((SLOTS, 8, 128), jnp.int32), pltpu.SemaphoreType.DMA((SLOTS,))],
        compiler_params=pltpu.CompilerParams(vmem_limit_bytes=4 * MIB),
    )(pltpu.with_memory_space_constraint(partner.reshape(-1, 128), pltpu.HBM))


def split_blocks(pieces):
    return [(piece, row) for piece in pieces for row in range(0, piece.shape[0], B)]


def sums_kernel(first, last, n_pieces, n_old, *refs):
    pieces = refs[:n_pieces]
    place_ref = refs[n_pieces]
    sums_in = refs[n_pieces + 1] if first > 0 else None
    sums_out, units_out, *part_out, sem = refs[n_pieces + (2 if first > 0 else 1) :]
    copies, done = [], 0
    for k, piece in enumerate(pieces[n_old:]):
        rows = piece.shape[0]
        copies.append(pltpu.make_async_copy(piece, units_out.at[pl.ds(done, rows), :], sem.at[k]))
        done += rows
    for copy in copies:
        copy.start()
    blocks = [piece[row : row + B, :] for piece, row in split_blocks(pieces)]
    rows = lax.broadcasted_iota(jnp.int32, (B, B), 0)
    lanes = lax.broadcasted_iota(jnp.int32, (B, B), 1)
    place = place_ref[...]

    def fold(value):
        return jnp.sum(value.reshape(-1, 8, B), axis=0)

    sums = [jnp.zeros((8, B), jnp.float32)] * last
    hits = jnp.zeros((8, B), jnp.float32)
    row_sums = {}
    for pair in range(first, last, 2):
        both = jnp.concatenate([blocks[pair], blocks[pair + 1]], axis=0)
        both_rows = lax.broadcasted_iota(jnp.int32, (2 * B, B), 0)
        both_total = jnp.zeros((2 * B, 128), jnp.float32)
        for c in range(first):
            raw = nt_dot(both, blocks[c])
            e = jnp.exp2(raw * SCALE)
            both_total = both_total + (e[:, :128] + e[:, 128:])
            sums[c] = sums[c] + fold(e)
            found = jnp.where(both_rows == place[c : c + 1, :] - pair * B, raw, 0.0)
            hits = hits + 2.0 * fold(found)
        for a in (pair, pair + 1):
            total = both_total[(a - pair) * B : (a - pair + 1) * B, :]
            for c in range(a, last):
                raw = nt_dot(blocks[a], blocks[c])
                e = jnp.exp2(raw * SCALE)
                if c == a:
                    e = jnp.where(rows == lanes, 0.0, e)
                total = total + (e[:, :128] + e[:, 128:])
                found = fold(jnp.where(rows == place[c : c + 1, :] - a * B, raw, 0.0))
                if c != a:
                    sums[c] = sums[c] + fold(e)
                    found = 2.0 * found
                hits = hits + found
            row_sums[a] = jnp.sum(total.T, axis=0, keepdims=True)
    for s in range(last):
        total = jnp.sum(sums[s], axis=0, keepdims=True)
        total = total + (sums_in[s : s + 1, :] if s < first else row_sums[s])
        sums_out[s : s + 1, :] = total
    if last < SLOTS:
        sums_out[last:SLOTS, :] = jnp.zeros((SLOTS - last, B), jnp.float32)
    if first > 0:
        hits = hits + sums_in[SLOTS:, :]
    sums_out[SLOTS:, :] = hits
    if last == SLOTS:
        logs = jnp.log(sums_out[:SLOTS, :])
        part = jnp.sum(logs, axis=0, keepdims=True) - jnp.sum(hits, axis=0, keepdims=True) * (1.0 / TAU)
        part = part[:, :128] + part[:, 128:]
        part_out[0][...] = jnp.broadcast_to(part[None], part_out[0].shape)
    for copy in copies:
        copy.wait()


def sums(first, last, old, new, place, state, dp_count):
    pairs = (last - first) * (last + first + 1) // 2
    operands = list(old) + list(new) + [place] + list(state)
    is_last = last == SLOTS
    return pl.pallas_call(
        functools.partial(sums_kernel, first, last, len(old) + len(new), len(old)),
        out_shape=(
            jax.ShapeDtypeStruct((SLOTS + 8, B), jnp.float32),
            pltpu.HBM(((last - first) * B, E), jnp.bfloat16),
        )
        + ((jax.ShapeDtypeStruct((dp_count, 1, 128), jnp.float32),) if is_last else ()),
        in_specs=[VMEM] * len(operands),
        out_specs=(VMEM, HBM) + ((VMEM,) if is_last else ()),
        scratch_shapes=[pltpu.SemaphoreType.DMA((len(new),))],
        compiler_params=pltpu.CompilerParams(vmem_limit_bytes=12 * MIB),
        cost_estimate=pl.CostEstimate(
            flops=pairs * 2 * B * B * E, bytes_accessed=last * B * E * 2, transcendentals=pairs * B * B
        ),
    )(*operands)


def grad_kernel(*refs):
    unit_refs = refs[: len(STAGES)]
    place_ref, totals_ref, emb_ref, grad_ref, units, sem = refs[len(STAGES) :]
    copies = []
    for k, (ref, row) in enumerate(split_blocks(unit_refs)):
        target = units.at[pl.ds(k * B, B), :]
        copies.append(pltpu.make_async_copy(ref.at[pl.ds(row, B), :], target, sem.at[k]))
    for copy in copies:
        copy.start()
    inverse = 1.0 / totals_ref[:SLOTS, :]
    row_inv = column(inverse[0:1, :])
    row_inv = jnp.concatenate([row_inv, row_inv], axis=1)
    place = jnp.concatenate([place_ref[...], place_ref[...]], axis=1)
    rows = lax.broadcasted_iota(jnp.int32, (B, B), 0)
    lanes = lax.broadcasted_iota(jnp.int32, (B, B), 1)
    emb = emb_ref[...]
    lengths = jnp.sqrt(jnp.sum(emb * emb, axis=1, keepdims=True) + 1e-06)
    unit = emb / lengths
    unit_grad = None
    for start in range(0, SLOTS * B, CHUNK):
        for copy in copies[start // B : (start + CHUNK) // B]:
            copy.wait()
        cols = units[start : start + CHUNK, :]
        raw = nt_dot(units[0:B, :], cols)
        row_w, col_w = [], []
        for k in range(CHUNK // B):
            b = start // B + k
            e = jnp.exp2(raw[:, k * B : (k + 1) * B] * SCALE)
            if b == 0:
                e = jnp.where(rows == lanes, 0.0, e)
            ind = jnp.where(lanes + b * B == place, 1.0, 0.0)
            row_w.append((e * row_inv - ind).astype(jnp.bfloat16))
            col_w.append((e * inverse[b : b + 1, :] - ind).astype(jnp.bfloat16))
        both = jnp.concatenate(
            [jnp.concatenate(row_w, axis=1), jnp.concatenate(col_w, axis=1)], axis=0
        )
        both = jnp.dot(both, cols, preferred_element_type=jnp.float32)
        part = both[:B] + both[B:]
        unit_grad = part if unit_grad is None else unit_grad + part
    unit_grad = unit_grad * (1.0 / TAU)
    along = jnp.sum(unit * unit_grad, axis=1, keepdims=True)
    grad_ref[...] = (unit_grad - unit * along) / lengths


def grads(units, place, totals, embeddings):
    return pl.pallas_call(
        grad_kernel,
        out_shape=jax.ShapeDtypeStruct((B, E), jnp.float32),
        in_specs=[HBM] * len(units) + [VMEM] * 3,
        out_specs=VMEM,
        scratch_shapes=[
            pltpu.VMEM((SLOTS * B, E), jnp.bfloat16),
            pltpu.SemaphoreType.DMA((SLOTS,)),
        ],
        compiler_params=pltpu.CompilerParams(vmem_limit_bytes=16 * MIB),
        cost_estimate=pl.CostEstimate(
            flops=6 * SLOTS * B * B * E, bytes_accessed=SLOTS * B * E * 2, transcendentals=SLOTS * B * B
        ),
    )(*[pltpu.with_memory_space_constraint(part, pltpu.HBM) for part in units], place, totals, embeddings)


def shift_x(value, step):
    dp_count = lax.axis_size("dp")
    perm = []
    for x in range(X):
        for z in range(Z):
            for k in range(dp_count):
                to_x = (x + (step if k % 2 == 0 else -step)) % X
                perm.append(((x * Z + z) * dp_count + k, (to_x * Z + z) * dp_count + k))
    return lax.ppermute(value, ("group", "dp"), perm)


def swap_z(value, mask):
    perm = [(x * Z + z, x * Z + (z ^ mask)) for x in range(X) for z in range(Z)]
    return lax.ppermute(value, "group", perm)


def stack_kernel(first_ref, second_ref, both_ref):
    both_ref[:B, :] = first_ref[...]
    both_ref[B:, :] = second_ref[...]


def stack(first, second):
    return pl.pallas_call(
        stack_kernel,
        out_shape=jax.ShapeDtypeStruct((2 * B, E), jnp.bfloat16),
        in_specs=[VMEM, VMEM],
        out_specs=VMEM,
        compiler_params=pltpu.CompilerParams(vmem_limit_bytes=4 * MIB),
    )(first, second)


def on_device(embeddings, partner):
    dp_count = lax.axis_size("dp")
    group_count = lax.axis_size("group")
    packed = pack(embeddings)
    place, own_place = places(partner, dp_count)

    z1 = swap_z(packed, 1)
    z2 = swap_z(packed, 2)
    near = stack(packed, z1)
    near_1, near_3 = shift_x(near, 1), shift_x(near, 3)
    z3, place, own_place = lax.optimization_barrier((swap_z(z2, 1), place, own_place))
    z2_1, z2_3 = shift_x(z2, 1), shift_x(z2, 3)
    z3_1, z3_3 = shift_x(z3, 1), shift_x(z3, 3)

    old, units, state = [], [], ()

    def add(*new):
        first, last = sum(STAGES[len(units) - 1 : len(units)]), STAGES[len(units)]
        part_sums, part_units, *rest = sums(first, last, old, new, place, state, dp_count)
        units.append(part_units)
        old.extend(new)
        return (part_sums,), rest

    near_1, near_3 = lax.optimization_barrier((near_1, near_3))
    near_2 = shift_x(near_1, 1)
    far_2 = shift_x(stack(z2_3, z3_3), 3)
    state, _ = add(near, z2, z3)
    state, _ = add(near_1, near_3)
    state, _ = add(z2_1, z3_1, z2_3, z3_3)
    state, _ = add(near_2)
    (totals,), (part,) = add(far_2)
    losses = lax.all_to_all(part, "dp", 0, 0)
    gradient = grads(units, own_place, totals, embeddings)
    loss = jnp.sum(losses) / (B * dp_count * group_count)
    return (gradient, loss)


def solution(mesh):
    placed = (P(("group", "dp"), None), P())
    return jax.shard_map(
        on_device,
        mesh=mesh,
        in_specs=placed,
        out_specs=(P(("group", "dp"), None), P()),
        check_vma=False,
    )
```

```python
import functools

import jax
import jax.numpy as jnp
from jax import lax
from jax.experimental import pallas as pl
from jax.experimental.pallas import tpu as pltpu
from jax.sharding import PartitionSpec as P

TAU = 0.1
LOG2E = 1.4426950408889634
SCALE = LOG2E / TAU
X = 4
Z = 4
B = 256
E = 512
SLOTS = X * Z
ORDER = [
    (0, 0), (0, 1), (0, 2), (0, 3),
    (1, 0), (1, 1), (3, 0), (3, 1),
    (1, 2), (1, 3), (3, 2), (3, 3),
    (2, 0), (2, 1),
    (2, 2), (2, 3),
]
STAGES = (4, 8, 12, 14, 16)
CHUNK = 1024
MIB = 1024 * 1024
VMEM = pl.BlockSpec(memory_space=pltpu.VMEM)
HBM = pl.BlockSpec(memory_space=pltpu.HBM)


def nt_dot(a, b):
    return lax.dot_general(a, b, (((1,), (1,)), ((), ())), preferred_element_type=jnp.float32)


def column(row):
    return jnp.broadcast_to(row, (128, B)).T


def pack_kernel(emb_ref, packed_ref):
    emb = emb_ref[...]
    lengths = jnp.sqrt(jnp.sum(emb * emb, axis=1, keepdims=True) + 1e-06)
    packed_ref[...] = (emb / lengths).astype(jnp.bfloat16)


def pack(embeddings):
    return pl.pallas_call(
        pack_kernel,
        out_shape=jax.ShapeDtypeStruct((B, E), jnp.bfloat16),
        in_specs=[VMEM],
        out_specs=VMEM,
        compiler_params=pltpu.CompilerParams(vmem_limit_bytes=4 * MIB),
    )(embeddings)


def owners():
    group_pos = lax.axis_index("group")
    own_x, own_z = lax.div(group_pos, Z), lax.rem(group_pos, Z)
    way = 1 - 2 * lax.rem(lax.axis_index("dp"), 2)
    return [((own_x - way * back_x) & (X - 1)) * Z + (own_z ^ mask) for back_x, mask in ORDER]


def place_kernel(dp_count, partner_ref, place_ref, own_ref, near, sem):
    group_pos = lax.axis_index("group")
    own_x, own_z = lax.div(group_pos, Z), lax.rem(group_pos, Z)
    lines = B // 128
    starts = [(owner * dp_count + lax.axis_index("dp")) * lines for owner in owners()]
    bases = [pl.multiple_of(lax.div(start, 8) * 8, 8) for start in starts]
    copies = [
        pltpu.make_async_copy(partner_ref.at[pl.ds(base, 8), :], near.at[k], sem.at[k])
        for k, base in enumerate(bases)
    ]
    for copy in copies:
        copy.start()
    for copy in copies:
        copy.wait()
    for s in range(SLOTS):
        for line in range(lines):
            row = near[s, pl.ds(starts[s] - bases[s] + line, 1), :]
            place_ref[s : s + 1, line * 128 : (line + 1) * 128] = row
    partner = place_ref[...]
    far = partner // (dp_count * B)
    way = 1 - 2 * lax.rem(lax.axis_index("dp"), 2)
    back = ((way * (own_x - far // Z)) & (X - 1)) * Z + ((far & (Z - 1)) ^ own_z)
    slot = jnp.zeros_like(back)
    for k, (back_x, mask) in enumerate(ORDER):
        slot = jnp.where(back == back_x * Z + mask, k, slot)
    place = slot * B + (partner & (B - 1))
    place_ref[...] = place
    own_ref[...] = column(place[0:1, :])


def places(partner, dp_count):
    return pl.pallas_call(
        functools.partial(place_kernel, dp_count),
        out_shape=(
            jax.ShapeDtypeStruct((SLOTS, B), jnp.int32),
            jax.ShapeDtypeStruct((B, 128), jnp.int32),
        ),
        in_specs=[HBM],
        out_specs=(VMEM, VMEM),
        scratch_shapes=[pltpu.VMEM((SLOTS, 8, 128), jnp.int32), pltpu.SemaphoreType.DMA((SLOTS,))],
        compiler_params=pltpu.CompilerParams(vmem_limit_bytes=4 * MIB),
    )(pltpu.with_memory_space_constraint(partner.reshape(-1, 128), pltpu.HBM))


def split_blocks(pieces):
    return [(piece, row) for piece in pieces for row in range(0, piece.shape[0], B)]


def sums_kernel(first, last, n_pieces, n_old, *refs):
    pieces = refs[:n_pieces]
    place_ref = refs[n_pieces]
    sums_in = refs[n_pieces + 1] if first > 0 else None
    sums_out, units_out, *part_out, sem = refs[n_pieces + (2 if first > 0 else 1) :]
    copies, done = [], 0
    for k, piece in enumerate(pieces[n_old:]):
        rows = piece.shape[0]
        copies.append(pltpu.make_async_copy(piece, units_out.at[pl.ds(done, rows), :], sem.at[k]))
        done += rows
    for copy in copies:
        copy.start()
    blocks = [piece[row : row + B, :] for piece, row in split_blocks(pieces)]
    rows = lax.broadcasted_iota(jnp.int32, (B, B), 0)
    lanes = lax.broadcasted_iota(jnp.int32, (B, B), 1)
    place = place_ref[...]

    def fold(value):
        return jnp.sum(value.reshape(-1, 8, B), axis=0)

    sums = [jnp.zeros((8, B), jnp.float32)] * last
    hits = jnp.zeros((8, B), jnp.float32)
    new = jnp.concatenate(blocks[first:], axis=0)
    new_rows = lax.broadcasted_iota(jnp.int32, (new.shape[0], B), 0) + first * B
    row_sums = [jnp.zeros((B, 128), jnp.float32)] * (last - first)
    for c in range(last):
        count = last - first if c < first else c - first + 1
        raw = nt_dot(new[: count * B, :], blocks[c])
        found = jnp.where(new_rows[: count * B, :] == place[c : c + 1, :], raw, 0.0)
        e = jnp.exp2(raw * SCALE)
        if c >= first:
            count -= 1
            own = jnp.where(rows == lanes, 0.0, e[count * B :, :])
            row_sums[count] = row_sums[count] + (own[:, :128] + own[:, 128:])
            hits = hits + fold(found[count * B :, :])
        if count > 0:
            sums[c] = fold(e[: count * B, :])
            hits = hits + 2.0 * fold(found[: count * B, :])
        for k in range(count):
            part = e[k * B : (k + 1) * B, :]
            row_sums[k] = row_sums[k] + (part[:, :128] + part[:, 128:])
    for s in range(last):
        total = jnp.sum(sums[s], axis=0, keepdims=True)
        if s < first:
            total = total + sums_in[s : s + 1, :]
        else:
            total = total + jnp.sum(row_sums[s - first].T, axis=0, keepdims=True)
        sums_out[s : s + 1, :] = total
    if last < SLOTS:
        sums_out[last:SLOTS, :] = jnp.zeros((SLOTS - last, B), jnp.float32)
    if first > 0:
        hits = hits + sums_in[SLOTS:, :]
    sums_out[SLOTS:, :] = hits
    if last == SLOTS:
        logs = jnp.log(sums_out[:SLOTS, :])
        part = jnp.sum(logs, axis=0, keepdims=True) - jnp.sum(hits, axis=0, keepdims=True) * (1.0 / TAU)
        part = part[:, :128] + part[:, 128:]
        part_out[0][...] = jnp.broadcast_to(part[None], part_out[0].shape)
    for copy in copies:
        copy.wait()


def sums(first, last, old, new, place, state, dp_count):
    pairs = (last - first) * (last + first + 1) // 2
    operands = list(old) + list(new) + [place] + list(state)
    is_last = last == SLOTS
    return pl.pallas_call(
        functools.partial(sums_kernel, first, last, len(old) + len(new), len(old)),
        out_shape=(
            jax.ShapeDtypeStruct((SLOTS + 8, B), jnp.float32),
            pltpu.HBM(((last - first) * B, E), jnp.bfloat16),
        )
        + ((jax.ShapeDtypeStruct((dp_count, 1, 128), jnp.float32),) if is_last else ()),
        in_specs=[VMEM] * len(operands),
        out_specs=(VMEM, HBM) + ((VMEM,) if is_last else ()),
        scratch_shapes=[pltpu.SemaphoreType.DMA((len(new),))],
        compiler_params=pltpu.CompilerParams(vmem_limit_bytes=12 * MIB),
        cost_estimate=pl.CostEstimate(
            flops=pairs * 2 * B * B * E, bytes_accessed=last * B * E * 2, transcendentals=pairs * B * B
        ),
    )(*operands)


def grad_kernel(*refs):
    unit_refs = refs[: len(STAGES)]
    place_ref, totals_ref, emb_ref, grad_ref, units, sem = refs[len(STAGES) :]
    copies = []
    for k, (ref, row) in enumerate(split_blocks(unit_refs)):
        target = units.at[pl.ds(k * B, B), :]
        copies.append(pltpu.make_async_copy(ref.at[pl.ds(row, B), :], target, sem.at[k]))
    for copy in copies:
        copy.start()
    inverse = 1.0 / totals_ref[:SLOTS, :]
    row_inv = column(inverse[0:1, :])
    row_inv = jnp.concatenate([row_inv, row_inv], axis=1)
    place = jnp.concatenate([place_ref[...], place_ref[...]], axis=1)
    rows = lax.broadcasted_iota(jnp.int32, (B, B), 0)
    lanes = lax.broadcasted_iota(jnp.int32, (B, B), 1)
    emb = emb_ref[...]
    lengths = jnp.sqrt(jnp.sum(emb * emb, axis=1, keepdims=True) + 1e-06)
    unit = emb / lengths
    unit_grad = None
    for start in range(0, SLOTS * B, CHUNK):
        for copy in copies[start // B : (start + CHUNK) // B]:
            copy.wait()
        cols = units[start : start + CHUNK, :]
        raw = nt_dot(units[0:B, :], cols)
        row_w, col_w = [], []
        for k in range(CHUNK // B):
            b = start // B + k
            e = jnp.exp2(raw[:, k * B : (k + 1) * B] * SCALE)
            if b == 0:
                e = jnp.where(rows == lanes, 0.0, e)
            ind = jnp.where(lanes + b * B == place, 1.0, 0.0)
            row_w.append((e * row_inv - ind).astype(jnp.bfloat16))
            col_w.append((e * inverse[b : b + 1, :] - ind).astype(jnp.bfloat16))
        both = jnp.concatenate(
            [jnp.concatenate(row_w, axis=1), jnp.concatenate(col_w, axis=1)], axis=0
        )
        both = jnp.dot(both, cols, preferred_element_type=jnp.float32)
        part = both[:B] + both[B:]
        unit_grad = part if unit_grad is None else unit_grad + part
    unit_grad = unit_grad * (1.0 / TAU)
    along = jnp.sum(unit * unit_grad, axis=1, keepdims=True)
    grad_ref[...] = (unit_grad - unit * along) / lengths


def grads(units, place, totals, embeddings):
    return pl.pallas_call(
        grad_kernel,
        out_shape=jax.ShapeDtypeStruct((B, E), jnp.float32),
        in_specs=[HBM] * len(units) + [VMEM] * 3,
        out_specs=VMEM,
        scratch_shapes=[
            pltpu.VMEM((SLOTS * B, E), jnp.bfloat16),
            pltpu.SemaphoreType.DMA((SLOTS,)),
        ],
        compiler_params=pltpu.CompilerParams(vmem_limit_bytes=16 * MIB),
        cost_estimate=pl.CostEstimate(
            flops=6 * SLOTS * B * B * E, bytes_accessed=SLOTS * B * E * 2, transcendentals=SLOTS * B * B
        ),
    )(*[pltpu.with_memory_space_constraint(part, pltpu.HBM) for part in units], place, totals, embeddings)


def shift_x(value, step):
    dp_count = lax.axis_size("dp")
    perm = []
    for x in range(X):
        for z in range(Z):
            for k in range(dp_count):
                to_x = (x + (step if k % 2 == 0 else -step)) % X
                perm.append(((x * Z + z) * dp_count + k, (to_x * Z + z) * dp_count + k))
    return lax.ppermute(value, ("group", "dp"), perm)


def swap_z(value, mask):
    perm = [(x * Z + z, x * Z + (z ^ mask)) for x in range(X) for z in range(Z)]
    return lax.ppermute(value, "group", perm)


def stack_kernel(first_ref, second_ref, both_ref):
    both_ref[:B, :] = first_ref[...]
    both_ref[B:, :] = second_ref[...]


def stack(first, second):
    return pl.pallas_call(
        stack_kernel,
        out_shape=jax.ShapeDtypeStruct((2 * B, E), jnp.bfloat16),
        in_specs=[VMEM, VMEM],
        out_specs=VMEM,
        compiler_params=pltpu.CompilerParams(vmem_limit_bytes=4 * MIB),
    )(first, second)


def on_device(embeddings, partner):
    dp_count = lax.axis_size("dp")
    group_count = lax.axis_size("group")
    packed = pack(embeddings)
    place, own_place = places(partner, dp_count)

    z1 = swap_z(packed, 1)
    z2 = swap_z(packed, 2)
    near = stack(packed, z1)
    near_1, near_3 = shift_x(near, 1), shift_x(near, 3)
    z3, place, own_place = lax.optimization_barrier((swap_z(z2, 1), place, own_place))
    z2_1, z2_3 = shift_x(z2, 1), shift_x(z2, 3)
    z3_1, z3_3 = shift_x(z3, 1), shift_x(z3, 3)

    old, units, state = [], [], ()

    def add(*new):
        first, last = sum(STAGES[len(units) - 1 : len(units)]), STAGES[len(units)]
        part_sums, part_units, *rest = sums(first, last, old, new, place, state, dp_count)
        units.append(part_units)
        old.extend(new)
        return (part_sums,), rest

    near_1, near_3, z2_1 = lax.optimization_barrier((near_1, near_3, z2_1))
    near_2 = shift_x(near_1, 1)
    far_pair = stack(z2_3, z3_3)
    far_pair, near = lax.optimization_barrier((far_pair, near))
    far_2 = shift_x(far_pair, 3)
    state, _ = add(near, z2, z3)
    state, _ = add(near_1, near_3)
    state, _ = add(z2_1, z3_1, z2_3, z3_3)
    state, _ = add(near_2)
    (totals,), (part,) = add(far_2)
    losses = lax.all_to_all(part, "dp", 0, 0)
    gradient = grads(units, own_place, totals, embeddings)
    loss = jnp.sum(losses) / (B * dp_count * group_count)
    return (gradient, loss)


def solution(mesh):
    placed = (P(("group", "dp"), None), P())
    return jax.shard_map(
        on_device,
        mesh=mesh,
        in_specs=placed,
        out_specs=(P(("group", "dp"), None), P()),
        check_vma=False,
    )
```

```python
import functools

import jax
import jax.numpy as jnp
from jax import lax
from jax.experimental import pallas as pl
from jax.experimental.pallas import tpu as pltpu
from jax.sharding import PartitionSpec as P

TAU = 0.1
LOG2E = 1.4426950408889634
SCALE = LOG2E / TAU
X = 4
Z = 4
B = 256
E = 512
SLOTS = X * Z
ORDER = [
    (0, 0), (0, 1), (0, 2), (0, 3),
    (1, 0), (1, 1), (3, 0), (3, 1),
    (1, 2), (1, 3), (3, 2), (3, 3),
    (2, 0), (2, 1),
    (2, 2), (2, 3),
]
STAGES = (8, 12, 14, 16)
CHUNK = 1024
MIB = 1024 * 1024
VMEM = pl.BlockSpec(memory_space=pltpu.VMEM)
HBM = pl.BlockSpec(memory_space=pltpu.HBM)


def nt_dot(a, b):
    return lax.dot_general(a, b, (((1,), (1,)), ((), ())), preferred_element_type=jnp.float32)


def column(row):
    return jnp.broadcast_to(row, (128, B)).T


def pack_kernel(emb_ref, packed_ref):
    emb = emb_ref[...]
    lengths = jnp.sqrt(jnp.sum(emb * emb, axis=1, keepdims=True) + 1e-06)
    packed_ref[...] = (emb / lengths).astype(jnp.bfloat16)


def pack(embeddings):
    return pl.pallas_call(
        pack_kernel,
        out_shape=jax.ShapeDtypeStruct((B, E), jnp.bfloat16),
        in_specs=[VMEM],
        out_specs=VMEM,
        compiler_params=pltpu.CompilerParams(vmem_limit_bytes=4 * MIB),
    )(embeddings)


def owners():
    group_pos = lax.axis_index("group")
    own_x, own_z = lax.div(group_pos, Z), lax.rem(group_pos, Z)
    way = 1 - 2 * lax.rem(lax.axis_index("dp"), 2)
    return [((own_x - way * back_x) & (X - 1)) * Z + (own_z ^ mask) for back_x, mask in ORDER]


def place_kernel(dp_count, partner_ref, place_ref, own_ref, near, sem):
    group_pos = lax.axis_index("group")
    own_x, own_z = lax.div(group_pos, Z), lax.rem(group_pos, Z)
    lines = B // 128
    starts = [(owner * dp_count + lax.axis_index("dp")) * lines for owner in owners()]
    bases = [pl.multiple_of(lax.div(start, 8) * 8, 8) for start in starts]
    copies = [
        pltpu.make_async_copy(partner_ref.at[pl.ds(base, 8), :], near.at[k], sem.at[k])
        for k, base in enumerate(bases)
    ]
    for copy in copies:
        copy.start()
    for copy in copies:
        copy.wait()
    for s in range(SLOTS):
        for line in range(lines):
            row = near[s, pl.ds(starts[s] - bases[s] + line, 1), :]
            place_ref[s : s + 1, line * 128 : (line + 1) * 128] = row
    partner = place_ref[...]
    far = partner // (dp_count * B)
    way = 1 - 2 * lax.rem(lax.axis_index("dp"), 2)
    back = ((way * (own_x - far // Z)) & (X - 1)) * Z + ((far & (Z - 1)) ^ own_z)
    slot = jnp.zeros_like(back)
    for k, (back_x, mask) in enumerate(ORDER):
        slot = jnp.where(back == back_x * Z + mask, k, slot)
    place = slot * B + (partner & (B - 1))
    place_ref[...] = place
    own_ref[...] = column(place[0:1, :])


def places(partner, dp_count):
    return pl.pallas_call(
        functools.partial(place_kernel, dp_count),
        out_shape=(
            jax.ShapeDtypeStruct((SLOTS, B), jnp.int32),
            jax.ShapeDtypeStruct((B, 128), jnp.int32),
        ),
        in_specs=[HBM],
        out_specs=(VMEM, VMEM),
        scratch_shapes=[pltpu.VMEM((SLOTS, 8, 128), jnp.int32), pltpu.SemaphoreType.DMA((SLOTS,))],
        compiler_params=pltpu.CompilerParams(vmem_limit_bytes=4 * MIB),
    )(pltpu.with_memory_space_constraint(partner.reshape(-1, 128), pltpu.HBM))


def split_blocks(pieces):
    return [(piece, row) for piece in pieces for row in range(0, piece.shape[0], B)]


def sums_kernel(first, last, n_pieces, n_old, *refs):
    pieces = refs[:n_pieces]
    place_ref = refs[n_pieces]
    sums_in = refs[n_pieces + 1] if first > 0 else None
    sums_out, units_out, *part_out, sem = refs[n_pieces + (2 if first > 0 else 1) :]
    copies, done = [], 0
    for k, piece in enumerate(pieces[n_old:]):
        rows = piece.shape[0]
        copies.append(pltpu.make_async_copy(piece, units_out.at[pl.ds(done, rows), :], sem.at[k]))
        done += rows
    for copy in copies:
        copy.start()
    blocks = [piece[row : row + B, :] for piece, row in split_blocks(pieces)]
    rows = lax.broadcasted_iota(jnp.int32, (B, B), 0)
    lanes = lax.broadcasted_iota(jnp.int32, (B, B), 1)
    place = place_ref[...]

    def fold(value):
        return jnp.sum(value.reshape(-1, 8, B), axis=0)

    sums = [jnp.zeros((8, B), jnp.float32)] * last
    hits = jnp.zeros((8, B), jnp.float32)
    new = jnp.concatenate(blocks[first:], axis=0)
    new_rows = lax.broadcasted_iota(jnp.int32, (new.shape[0], B), 0) + first * B
    row_sums = [jnp.zeros((B, 128), jnp.float32)] * (last - first)
    for c in range(last):
        count = last - first if c < first else c - first + 1
        raw = nt_dot(new[: count * B, :], blocks[c])
        found = jnp.where(new_rows[: count * B, :] == place[c : c + 1, :], raw, 0.0)
        e = jnp.exp2(raw * SCALE)
        if c >= first:
            count -= 1
            own = jnp.where(rows == lanes, 0.0, e[count * B :, :])
            row_sums[count] = row_sums[count] + (own[:, :128] + own[:, 128:])
            hits = hits + fold(found[count * B :, :])
        if count > 0:
            sums[c] = fold(e[: count * B, :])
            hits = hits + 2.0 * fold(found[: count * B, :])
        for k in range(count):
            part = e[k * B : (k + 1) * B, :]
            row_sums[k] = row_sums[k] + (part[:, :128] + part[:, 128:])
    for s in range(last):
        total = jnp.sum(sums[s], axis=0, keepdims=True)
        if s < first:
            total = total + sums_in[s : s + 1, :]
        else:
            total = total + jnp.sum(row_sums[s - first].T, axis=0, keepdims=True)
        sums_out[s : s + 1, :] = total
    if last < SLOTS:
        sums_out[last:SLOTS, :] = jnp.zeros((SLOTS - last, B), jnp.float32)
    if first > 0:
        hits = hits + sums_in[SLOTS:, :]
    sums_out[SLOTS:, :] = hits
    if last == SLOTS:
        logs = jnp.log(sums_out[:SLOTS, :])
        part = jnp.sum(logs, axis=0, keepdims=True) - jnp.sum(hits, axis=0, keepdims=True) * (1.0 / TAU)
        part = part[:, :128] + part[:, 128:]
        part_out[0][...] = jnp.broadcast_to(part[None], part_out[0].shape)
    for copy in copies:
        copy.wait()


def sums(first, last, old, new, place, state, dp_count):
    pairs = (last - first) * (last + first + 1) // 2
    operands = list(old) + list(new) + [place] + list(state)
    is_last = last == SLOTS
    return pl.pallas_call(
        functools.partial(sums_kernel, first, last, len(old) + len(new), len(old)),
        out_shape=(
            jax.ShapeDtypeStruct((SLOTS + 8, B), jnp.float32),
            pltpu.HBM(((last - first) * B, E), jnp.bfloat16),
        )
        + ((jax.ShapeDtypeStruct((dp_count, 1, 128), jnp.float32),) if is_last else ()),
        in_specs=[VMEM] * len(operands),
        out_specs=(VMEM, HBM) + ((VMEM,) if is_last else ()),
        scratch_shapes=[pltpu.SemaphoreType.DMA((len(new),))],
        compiler_params=pltpu.CompilerParams(vmem_limit_bytes=12 * MIB),
        cost_estimate=pl.CostEstimate(
            flops=pairs * 2 * B * B * E, bytes_accessed=last * B * E * 2, transcendentals=pairs * B * B
        ),
    )(*operands)


def grad_kernel(*refs):
    unit_refs = refs[: len(STAGES)]
    place_ref, totals_ref, emb_ref, grad_ref, units, sem = refs[len(STAGES) :]
    copies = []
    for k, (ref, row) in enumerate(split_blocks(unit_refs)):
        target = units.at[pl.ds(k * B, B), :]
        copies.append(pltpu.make_async_copy(ref.at[pl.ds(row, B), :], target, sem.at[k]))
    for copy in copies:
        copy.start()
    inverse = 1.0 / totals_ref[:SLOTS, :]
    row_inv = column(inverse[0:1, :])
    row_inv = jnp.concatenate([row_inv, row_inv], axis=1)
    place = jnp.concatenate([place_ref[...], place_ref[...]], axis=1)
    rows = lax.broadcasted_iota(jnp.int32, (B, B), 0)
    lanes = lax.broadcasted_iota(jnp.int32, (B, B), 1)
    emb = emb_ref[...]
    lengths = jnp.sqrt(jnp.sum(emb * emb, axis=1, keepdims=True) + 1e-06)
    unit = emb / lengths
    unit_grad = None
    for start in range(0, SLOTS * B, CHUNK):
        for copy in copies[start // B : (start + CHUNK) // B]:
            copy.wait()
        cols = units[start : start + CHUNK, :]
        raw = nt_dot(units[0:B, :], cols)
        row_w, col_w = [], []
        for k in range(CHUNK // B):
            b = start // B + k
            e = jnp.exp2(raw[:, k * B : (k + 1) * B] * SCALE)
            if b == 0:
                e = jnp.where(rows == lanes, 0.0, e)
            ind = jnp.where(lanes + b * B == place, 1.0, 0.0)
            row_w.append((e * row_inv - ind).astype(jnp.bfloat16))
            col_w.append((e * inverse[b : b + 1, :] - ind).astype(jnp.bfloat16))
        both = jnp.concatenate(
            [jnp.concatenate(row_w, axis=1), jnp.concatenate(col_w, axis=1)], axis=0
        )
        both = jnp.dot(both, cols, preferred_element_type=jnp.float32)
        part = both[:B] + both[B:]
        unit_grad = part if unit_grad is None else unit_grad + part
    unit_grad = unit_grad * (1.0 / TAU)
    along = jnp.sum(unit * unit_grad, axis=1, keepdims=True)
    grad_ref[...] = (unit_grad - unit * along) / lengths


def grads(units, place, totals, embeddings):
    return pl.pallas_call(
        grad_kernel,
        out_shape=jax.ShapeDtypeStruct((B, E), jnp.float32),
        in_specs=[HBM] * len(units) + [VMEM] * 3,
        out_specs=VMEM,
        scratch_shapes=[
            pltpu.VMEM((SLOTS * B, E), jnp.bfloat16),
            pltpu.SemaphoreType.DMA((SLOTS,)),
        ],
        compiler_params=pltpu.CompilerParams(vmem_limit_bytes=16 * MIB),
        cost_estimate=pl.CostEstimate(
            flops=6 * SLOTS * B * B * E, bytes_accessed=SLOTS * B * E * 2, transcendentals=SLOTS * B * B
        ),
    )(*[pltpu.with_memory_space_constraint(part, pltpu.HBM) for part in units], place, totals, embeddings)


def shift_x(value, step):
    dp_count = lax.axis_size("dp")
    perm = []
    for x in range(X):
        for z in range(Z):
            for k in range(dp_count):
                to_x = (x + (step if k % 2 == 0 else -step)) % X
                perm.append(((x * Z + z) * dp_count + k, (to_x * Z + z) * dp_count + k))
    return lax.ppermute(value, ("group", "dp"), perm)


def swap_z(value, mask):
    perm = [(x * Z + z, x * Z + (z ^ mask)) for x in range(X) for z in range(Z)]
    return lax.ppermute(value, "group", perm)


def stack_kernel(first_ref, second_ref, both_ref):
    both_ref[:B, :] = first_ref[...]
    both_ref[B:, :] = second_ref[...]


def stack(first, second):
    return pl.pallas_call(
        stack_kernel,
        out_shape=jax.ShapeDtypeStruct((2 * B, E), jnp.bfloat16),
        in_specs=[VMEM, VMEM],
        out_specs=VMEM,
        compiler_params=pltpu.CompilerParams(vmem_limit_bytes=4 * MIB),
    )(first, second)


def on_device(embeddings, partner):
    dp_count = lax.axis_size("dp")
    group_count = lax.axis_size("group")
    packed = pack(embeddings)
    place, own_place = places(partner, dp_count)

    z1, place, own_place = lax.optimization_barrier((swap_z(packed, 1), place, own_place))
    z2 = swap_z(packed, 2)
    near = stack(packed, z1)
    near_1, near_3 = shift_x(near, 1), shift_x(near, 3)
    z3 = swap_z(z2, 1)
    z2_1, z2_3 = shift_x(z2, 1), shift_x(z2, 3)
    z3_1, z3_3 = shift_x(z3, 1), shift_x(z3, 3)

    old, units, state = [], [], ()

    def add(*new):
        first, last = sum(STAGES[len(units) - 1 : len(units)]), STAGES[len(units)]
        part_sums, part_units, *rest = sums(first, last, old, new, place, state, dp_count)
        units.append(part_units)
        old.extend(new)
        return (part_sums,), rest

    near_1, near_3, z2_1 = lax.optimization_barrier((near_1, near_3, z2_1))
    near_2 = shift_x(near_1, 1)
    far_pair = stack(z2_3, z3_3)
    far_pair, near = lax.optimization_barrier((far_pair, near))
    far_2 = shift_x(far_pair, 3)
    state, _ = add(near, z2, z3, near_1, near_3)
    state, _ = add(z2_1, z3_1, z2_3, z3_3)
    state, _ = add(near_2)
    (totals,), (part,) = add(far_2)
    losses = lax.all_to_all(part, "dp", 0, 0)
    gradient = grads(units, own_place, totals, embeddings)
    loss = jnp.sum(losses) / (B * dp_count * group_count)
    return (gradient, loss)


def solution(mesh):
    placed = (P(("group", "dp"), None), P())
    return jax.shard_map(
        on_device,
        mesh=mesh,
        in_specs=placed,
        out_specs=(P(("group", "dp"), None), P()),
        check_vma=False,
    )
```

```python
import functools

import jax
import jax.numpy as jnp
from jax import lax
from jax.experimental import pallas as pl
from jax.experimental.pallas import tpu as pltpu
from jax.sharding import PartitionSpec as P

TAU = 0.1
LOG2E = 1.4426950408889634
SCALE = LOG2E / TAU
X = 4
Z = 4
B = 256
E = 512
SLOTS = X * Z
ORDER = [
    (0, 0), (0, 1), (0, 2), (0, 3),
    (1, 0), (1, 1), (3, 0), (3, 1),
    (1, 2), (1, 3), (3, 2), (3, 3),
    (2, 0), (2, 1),
    (2, 2), (2, 3),
]
STAGES = (4, 8, 12, 14, 16)
CHUNK = 1024
MIB = 1024 * 1024
VMEM = pl.BlockSpec(memory_space=pltpu.VMEM)
HBM = pl.BlockSpec(memory_space=pltpu.HBM)


def nt_dot(a, b):
    return lax.dot_general(a, b, (((1,), (1,)), ((), ())), preferred_element_type=jnp.float32)


def column(row):
    return jnp.broadcast_to(row, (128, B)).T


def pack_kernel(emb_ref, packed_ref):
    emb = emb_ref[...]
    lengths = jnp.sqrt(jnp.sum(emb * emb, axis=1, keepdims=True) + 1e-06)
    packed_ref[...] = (emb / lengths).astype(jnp.bfloat16)


def pack(embeddings):
    return pl.pallas_call(
        pack_kernel,
        out_shape=jax.ShapeDtypeStruct((B, E), jnp.bfloat16),
        in_specs=[VMEM],
        out_specs=VMEM,
        compiler_params=pltpu.CompilerParams(vmem_limit_bytes=4 * MIB),
    )(embeddings)


def owners():
    group_pos = lax.axis_index("group")
    own_x, own_z = lax.div(group_pos, Z), lax.rem(group_pos, Z)
    way = 1 - 2 * lax.rem(lax.axis_index("dp"), 2)
    return [((own_x - way * back_x) & (X - 1)) * Z + (own_z ^ mask) for back_x, mask in ORDER]


def place_kernel(dp_count, partner_ref, place_ref, own_ref, near, sem):
    group_pos = lax.axis_index("group")
    own_x, own_z = lax.div(group_pos, Z), lax.rem(group_pos, Z)
    lines = B // 128
    starts = [(owner * dp_count + lax.axis_index("dp")) * lines for owner in owners()]
    bases = [pl.multiple_of(lax.div(start, 8) * 8, 8) for start in starts]
    copies = [
        pltpu.make_async_copy(partner_ref.at[pl.ds(base, 8), :], near.at[k], sem.at[k])
        for k, base in enumerate(bases)
    ]
    for copy in copies:
        copy.start()
    for copy in copies:
        copy.wait()
    for s in range(SLOTS):
        for line in range(lines):
            row = near[s, pl.ds(starts[s] - bases[s] + line, 1), :]
            place_ref[s : s + 1, line * 128 : (line + 1) * 128] = row
    partner = place_ref[...]
    far = partner // (dp_count * B)
    way = 1 - 2 * lax.rem(lax.axis_index("dp"), 2)
    back = ((way * (own_x - far // Z)) & (X - 1)) * Z + ((far & (Z - 1)) ^ own_z)
    slot = jnp.zeros_like(back)
    for k, (back_x, mask) in enumerate(ORDER):
        slot = jnp.where(back == back_x * Z + mask, k, slot)
    place = slot * B + (partner & (B - 1))
    place_ref[...] = place
    own_ref[...] = column(place[0:1, :])


def places(partner, dp_count):
    return pl.pallas_call(
        functools.partial(place_kernel, dp_count),
        out_shape=(
            jax.ShapeDtypeStruct((SLOTS, B), jnp.int32),
            jax.ShapeDtypeStruct((B, 128), jnp.int32),
        ),
        in_specs=[HBM],
        out_specs=(VMEM, VMEM),
        scratch_shapes=[pltpu.VMEM((SLOTS, 8, 128), jnp.int32), pltpu.SemaphoreType.DMA((SLOTS,))],
        compiler_params=pltpu.CompilerParams(vmem_limit_bytes=4 * MIB),
    )(pltpu.with_memory_space_constraint(partner.reshape(-1, 128), pltpu.HBM))


def split_blocks(pieces):
    return [(piece, row) for piece in pieces for row in range(0, piece.shape[0], B)]


def sums_kernel(first, last, n_pieces, n_old, *refs):
    pieces = refs[:n_pieces]
    place_ref = refs[n_pieces]
    sums_in = refs[n_pieces + 1] if first > 0 else None
    sums_out, units_out, *part_out, sem = refs[n_pieces + (2 if first > 0 else 1) :]
    copies, done = [], 0
    for k, piece in enumerate(pieces[n_old:]):
        rows = piece.shape[0]
        copies.append(pltpu.make_async_copy(piece, units_out.at[pl.ds(done, rows), :], sem.at[k]))
        done += rows
    for copy in copies:
        copy.start()
    blocks = [piece[row : row + B, :] for piece, row in split_blocks(pieces)]
    rows = lax.broadcasted_iota(jnp.int32, (B, B), 0)
    lanes = lax.broadcasted_iota(jnp.int32, (B, B), 1)
    place = place_ref[...]

    def fold(value):
        return jnp.sum(value.reshape(-1, 8, B), axis=0)

    sums = [jnp.zeros((8, B), jnp.float32)] * last
    hits = jnp.zeros((8, B), jnp.float32)
    new = jnp.concatenate(blocks[first:], axis=0)
    new_rows = lax.broadcasted_iota(jnp.int32, (new.shape[0], B), 0) + first * B
    row_sums = [jnp.zeros((B, 128), jnp.float32)] * (last - first)
    for c in range(last):
        count = last - first if c < first else c - first + 1
        raw = nt_dot(new[: count * B, :], blocks[c])
        found = jnp.where(new_rows[: count * B, :] == place[c : c + 1, :], raw, 0.0)
        e = jnp.exp2(raw * SCALE)
        if c >= first:
            count -= 1
            own = jnp.where(rows == lanes, 0.0, e[count * B :, :])
            row_sums[count] = row_sums[count] + (own[:, :128] + own[:, 128:])
            hits = hits + fold(found[count * B :, :])
        if count > 0:
            sums[c] = fold(e[: count * B, :])
            hits = hits + 2.0 * fold(found[: count * B, :])
        for k in range(count):
            part = e[k * B : (k + 1) * B, :]
            row_sums[k] = row_sums[k] + (part[:, :128] + part[:, 128:])
    for s in range(last):
        total = jnp.sum(sums[s], axis=0, keepdims=True)
        if s < first:
            total = total + sums_in[s : s + 1, :]
        else:
            total = total + jnp.sum(row_sums[s - first].T, axis=0, keepdims=True)
        sums_out[s : s + 1, :] = total
    if last < SLOTS:
        sums_out[last:SLOTS, :] = jnp.zeros((SLOTS - last, B), jnp.float32)
    if first > 0:
        hits = hits + sums_in[SLOTS:, :]
    sums_out[SLOTS:, :] = hits
    if last == SLOTS:
        logs = jnp.log(sums_out[:SLOTS, :])
        part = jnp.sum(logs, axis=0, keepdims=True) - jnp.sum(hits, axis=0, keepdims=True) * (1.0 / TAU)
        part = part[:, :128] + part[:, 128:]
        part_out[0][...] = jnp.broadcast_to(part[None], part_out[0].shape)
    for copy in copies:
        copy.wait()


def sums(first, last, old, new, place, state, dp_count):
    pairs = (last - first) * (last + first + 1) // 2
    operands = list(old) + list(new) + [place] + list(state)
    is_last = last == SLOTS
    return pl.pallas_call(
        functools.partial(sums_kernel, first, last, len(old) + len(new), len(old)),
        out_shape=(
            jax.ShapeDtypeStruct((SLOTS + 8, B), jnp.float32),
            pltpu.HBM(((last - first) * B, E), jnp.bfloat16),
        )
        + ((jax.ShapeDtypeStruct((dp_count, 1, 128), jnp.float32),) if is_last else ()),
        in_specs=[VMEM] * len(operands),
        out_specs=(VMEM, HBM) + ((VMEM,) if is_last else ()),
        scratch_shapes=[pltpu.SemaphoreType.DMA((len(new),))],
        compiler_params=pltpu.CompilerParams(vmem_limit_bytes=12 * MIB),
        cost_estimate=pl.CostEstimate(
            flops=pairs * 2 * B * B * E, bytes_accessed=last * B * E * 2, transcendentals=pairs * B * B
        ),
    )(*operands)


def grad_kernel(*refs):
    unit_refs = refs[: len(STAGES)]
    place_ref, totals_ref, emb_ref, grad_ref, units, sem = refs[len(STAGES) :]
    copies = []
    for k, (ref, row) in enumerate(split_blocks(unit_refs)):
        target = units.at[pl.ds(k * B, B), :]
        copies.append(pltpu.make_async_copy(ref.at[pl.ds(row, B), :], target, sem.at[k]))
    for copy in copies:
        copy.start()
    inverse = 1.0 / totals_ref[:SLOTS, :]
    row_inv = column(inverse[0:1, :])
    row_inv = jnp.concatenate([row_inv, row_inv], axis=1)
    place = jnp.concatenate([place_ref[...], place_ref[...]], axis=1)
    rows = lax.broadcasted_iota(jnp.int32, (B, B), 0)
    lanes = lax.broadcasted_iota(jnp.int32, (B, B), 1)
    emb = emb_ref[...]
    lengths = jnp.sqrt(jnp.sum(emb * emb, axis=1, keepdims=True) + 1e-06)
    unit = emb / lengths
    unit_grad = None
    for start in range(0, SLOTS * B, CHUNK):
        for copy in copies[start // B : (start + CHUNK) // B]:
            copy.wait()
        cols = units[start : start + CHUNK, :]
        raw = nt_dot(units[0:B, :], cols)
        row_w, col_w = [], []
        for k in range(CHUNK // B):
            b = start // B + k
            e = jnp.exp2(raw[:, k * B : (k + 1) * B] * SCALE)
            if b == 0:
                e = jnp.where(rows == lanes, 0.0, e)
            ind = jnp.where(lanes + b * B == place, 1.0, 0.0)
            row_w.append((e * row_inv - ind).astype(jnp.bfloat16))
            col_w.append((e * inverse[b : b + 1, :] - ind).astype(jnp.bfloat16))
        both = jnp.concatenate(
            [jnp.concatenate(row_w, axis=1), jnp.concatenate(col_w, axis=1)], axis=0
        )
        both = jnp.dot(both, cols, preferred_element_type=jnp.float32)
        part = both[:B] + both[B:]
        unit_grad = part if unit_grad is None else unit_grad + part
    unit_grad = unit_grad * (1.0 / TAU)
    along = jnp.sum(unit * unit_grad, axis=1, keepdims=True)
    grad_ref[...] = (unit_grad - unit * along) / lengths


def grads(units, place, totals, embeddings):
    return pl.pallas_call(
        grad_kernel,
        out_shape=jax.ShapeDtypeStruct((B, E), jnp.float32),
        in_specs=[HBM] * len(units) + [VMEM] * 3,
        out_specs=VMEM,
        scratch_shapes=[
            pltpu.VMEM((SLOTS * B, E), jnp.bfloat16),
            pltpu.SemaphoreType.DMA((SLOTS,)),
        ],
        compiler_params=pltpu.CompilerParams(vmem_limit_bytes=16 * MIB),
        cost_estimate=pl.CostEstimate(
            flops=6 * SLOTS * B * B * E, bytes_accessed=SLOTS * B * E * 2, transcendentals=SLOTS * B * B
        ),
    )(*[pltpu.with_memory_space_constraint(part, pltpu.HBM) for part in units], place, totals, embeddings)


def shift_x(value, step):
    dp_count = lax.axis_size("dp")
    perm = []
    for x in range(X):
        for z in range(Z):
            for k in range(dp_count):
                to_x = (x + (step if k % 2 == 0 else -step)) % X
                perm.append(((x * Z + z) * dp_count + k, (to_x * Z + z) * dp_count + k))
    return lax.ppermute(value, ("group", "dp"), perm)


def loss_groups(dp_count):
    segments = ((3, 3, 0, 0), (0, 0, 3, 3), (1, 1, 2, 2), (2, 2, 1, 1))
    return [
        [(x * Z + lows[k // 2 % 4]) * dp_count + k for k in range(dp_count)]
        for x in range(X)
        for lows in segments
    ]


def swap_z(value, mask):
    perm = [(x * Z + z, x * Z + (z ^ mask)) for x in range(X) for z in range(Z)]
    return lax.ppermute(value, "group", perm)


def stack_kernel(first_ref, second_ref, both_ref):
    both_ref[:B, :] = first_ref[...]
    both_ref[B:, :] = second_ref[...]


def stack(first, second):
    return pl.pallas_call(
        stack_kernel,
        out_shape=jax.ShapeDtypeStruct((2 * B, E), jnp.bfloat16),
        in_specs=[VMEM, VMEM],
        out_specs=VMEM,
        compiler_params=pltpu.CompilerParams(vmem_limit_bytes=4 * MIB),
    )(first, second)


def on_device(embeddings, partner):
    dp_count = lax.axis_size("dp")
    group_count = lax.axis_size("group")
    packed = pack(embeddings)
    place, own_place = places(partner, dp_count)

    z1 = swap_z(packed, 1)
    z2 = swap_z(packed, 2)
    near = stack(packed, z1)
    near_1, near_3 = shift_x(near, 1), shift_x(near, 3)
    z3, place, own_place = lax.optimization_barrier((swap_z(z2, 1), place, own_place))
    z2_1, z2_3 = shift_x(z2, 1), shift_x(z2, 3)
    z3_1, z3_3 = shift_x(z3, 1), shift_x(z3, 3)

    old, units, state = [], [], ()

    def add(*new):
        first, last = sum(STAGES[len(units) - 1 : len(units)]), STAGES[len(units)]
        part_sums, part_units, *rest = sums(first, last, old, new, place, state, dp_count)
        units.append(part_units)
        old.extend(new)
        return (part_sums,), rest

    near_1, near_3, z2_1 = lax.optimization_barrier((near_1, near_3, z2_1))
    near_2 = shift_x(near_1, 1)
    far_pair = stack(z2_3, z3_3)
    far_pair, near = lax.optimization_barrier((far_pair, near))
    far_2 = shift_x(far_pair, 3)
    state, _ = add(near, z2, z3)
    state, _ = add(near_1, near_3)
    state, _ = add(z2_1, z3_1, z2_3, z3_3)
    state, _ = add(near_2)
    (totals,), (part,) = add(far_2)
    losses = lax.all_to_all(part, ("group", "dp"), 0, 0, axis_index_groups=loss_groups(dp_count))
    gradient = grads(units, own_place, totals, embeddings)
    loss = jnp.sum(losses) / (B * dp_count * group_count)
    return (gradient, loss)


def solution(mesh):
    placed = (P(("group", "dp"), None), P())
    return jax.shard_map(
        on_device,
        mesh=mesh,
        in_specs=placed,
        out_specs=(P(("group", "dp"), None), P()),
        check_vma=False,
    )
```

```python
import functools

import jax
import jax.numpy as jnp
from jax import lax
from jax.experimental import pallas as pl
from jax.experimental.pallas import tpu as pltpu
from jax.sharding import PartitionSpec as P

TAU = 0.1
LOG2E = 1.4426950408889634
SCALE = LOG2E / TAU
X = 4
Z = 4
B = 256
E = 512
SLOTS = X * Z
ORDER = [
    (0, 0), (0, 1), (0, 2), (0, 3),
    (1, 0), (1, 1), (3, 0), (3, 1),
    (1, 2), (1, 3), (3, 2), (3, 3),
    (2, 0), (2, 1),
    (2, 2), (2, 3),
]
STAGES = (4, 8, 12, 14, 16)
CHUNK = 1024
MIB = 1024 * 1024
VMEM = pl.BlockSpec(memory_space=pltpu.VMEM)
HBM = pl.BlockSpec(memory_space=pltpu.HBM)


def nt_dot(a, b):
    return lax.dot_general(a, b, (((1,), (1,)), ((), ())), preferred_element_type=jnp.float32)


def column(row):
    return jnp.broadcast_to(row, (128, B)).T


def pack_kernel(emb_ref, packed_ref):
    emb = emb_ref[...]
    lengths = jnp.sqrt(jnp.sum(emb * emb, axis=1, keepdims=True) + 1e-06)
    packed_ref[...] = (emb / lengths).astype(jnp.bfloat16)


def pack(embeddings):
    return pl.pallas_call(
        pack_kernel,
        out_shape=jax.ShapeDtypeStruct((B, E), jnp.bfloat16),
        in_specs=[VMEM],
        out_specs=VMEM,
        compiler_params=pltpu.CompilerParams(vmem_limit_bytes=4 * MIB),
    )(embeddings)


def owners():
    group_pos = lax.axis_index("group")
    own_x, own_z = lax.div(group_pos, Z), lax.rem(group_pos, Z)
    way = 1 - 2 * lax.rem(lax.axis_index("dp"), 2)
    return [((own_x - way * back_x) & (X - 1)) * Z + (own_z ^ mask) for back_x, mask in ORDER]


def place_kernel(dp_count, partner_ref, place_ref, own_ref, near, sem):
    group_pos = lax.axis_index("group")
    own_x, own_z = lax.div(group_pos, Z), lax.rem(group_pos, Z)
    lines = B // 128
    starts = [(owner * dp_count + lax.axis_index("dp")) * lines for owner in owners()]
    bases = [pl.multiple_of(lax.div(start, 8) * 8, 8) for start in starts]
    copies = [
        pltpu.make_async_copy(partner_ref.at[pl.ds(base, 8), :], near.at[k], sem.at[k])
        for k, base in enumerate(bases)
    ]
    for copy in copies:
        copy.start()
    for copy in copies:
        copy.wait()
    for s in range(SLOTS):
        for line in range(lines):
            row = near[s, pl.ds(starts[s] - bases[s] + line, 1), :]
            place_ref[s : s + 1, line * 128 : (line + 1) * 128] = row
    partner = place_ref[...]
    far = partner // (dp_count * B)
    way = 1 - 2 * lax.rem(lax.axis_index("dp"), 2)
    back = ((way * (own_x - far // Z)) & (X - 1)) * Z + ((far & (Z - 1)) ^ own_z)
    slot = jnp.zeros_like(back)
    for k, (back_x, mask) in enumerate(ORDER):
        slot = jnp.where(back == back_x * Z + mask, k, slot)
    place = slot * B + (partner & (B - 1))
    place_ref[...] = place
    own_ref[...] = column(place[0:1, :])


def places(partner, dp_count):
    return pl.pallas_call(
        functools.partial(place_kernel, dp_count),
        out_shape=(
            jax.ShapeDtypeStruct((SLOTS, B), jnp.int32),
            jax.ShapeDtypeStruct((B, 128), jnp.int32),
        ),
        in_specs=[HBM],
        out_specs=(VMEM, VMEM),
        scratch_shapes=[pltpu.VMEM((SLOTS, 8, 128), jnp.int32), pltpu.SemaphoreType.DMA((SLOTS,))],
        compiler_params=pltpu.CompilerParams(vmem_limit_bytes=4 * MIB),
    )(pltpu.with_memory_space_constraint(partner.reshape(-1, 128), pltpu.HBM))


def split_blocks(pieces):
    return [(piece, row) for piece in pieces for row in range(0, piece.shape[0], B)]


def sums_kernel(first, last, n_pieces, n_old, *refs):
    pieces = refs[:n_pieces]
    place_ref = refs[n_pieces]
    sums_in = refs[n_pieces + 1] if first > 0 else None
    sums_out, units_out, *part_out, sem = refs[n_pieces + (2 if first > 0 else 1) :]
    copies, done = [], 0
    for k, piece in enumerate(pieces[n_old:]):
        rows = piece.shape[0]
        copies.append(pltpu.make_async_copy(piece, units_out.at[pl.ds(done, rows), :], sem.at[k]))
        done += rows
    for copy in copies:
        copy.start()
    blocks = [piece[row : row + B, :] for piece, row in split_blocks(pieces)]
    rows = lax.broadcasted_iota(jnp.int32, (B, B), 0)
    lanes = lax.broadcasted_iota(jnp.int32, (B, B), 1)
    place = place_ref[...]

    def fold(value):
        return jnp.sum(value.reshape(-1, 8, B), axis=0)

    sums = [jnp.zeros((8, B), jnp.float32)] * last
    hits = jnp.zeros((8, B), jnp.float32)
    new = jnp.concatenate(blocks[first:], axis=0)
    new_rows = lax.broadcasted_iota(jnp.int32, (new.shape[0], B), 0) + first * B
    row_sums = [jnp.zeros((B, 128), jnp.float32)] * (last - first)
    for c in range(last):
        count = last - first if c < first else c - first + 1
        raw = nt_dot(new[: count * B, :], blocks[c])
        found = jnp.where(new_rows[: count * B, :] == place[c : c + 1, :], raw, 0.0)
        e = jnp.exp2(raw * SCALE)
        if c >= first:
            count -= 1
            own = jnp.where(rows == lanes, 0.0, e[count * B :, :])
            row_sums[count] = row_sums[count] + (own[:, :128] + own[:, 128:])
            hits = hits + fold(found[count * B :, :])
        if count > 0:
            sums[c] = fold(e[: count * B, :])
            hits = hits + 2.0 * fold(found[: count * B, :])
        for k in range(count):
            part = e[k * B : (k + 1) * B, :]
            row_sums[k] = row_sums[k] + (part[:, :128] + part[:, 128:])
    for s in range(last):
        total = jnp.sum(sums[s], axis=0, keepdims=True)
        if s < first:
            total = total + sums_in[s : s + 1, :]
        else:
            total = total + jnp.sum(row_sums[s - first].T, axis=0, keepdims=True)
        sums_out[s : s + 1, :] = total
    if last < SLOTS:
        sums_out[last:SLOTS, :] = jnp.zeros((SLOTS - last, B), jnp.float32)
    if first > 0:
        hits = hits + sums_in[SLOTS:, :]
    sums_out[SLOTS:, :] = hits
    if last == SLOTS:
        logs = jnp.log(sums_out[:SLOTS, :])
        part = jnp.sum(logs, axis=0, keepdims=True) - jnp.sum(hits, axis=0, keepdims=True) * (1.0 / TAU)
        part = part[:, :128] + part[:, 128:]
        part_out[0][...] = jnp.broadcast_to(part[None], part_out[0].shape)
    for copy in copies:
        copy.wait()


def sums(first, last, old, new, place, state, dp_count):
    pairs = (last - first) * (last + first + 1) // 2
    operands = list(old) + list(new) + [place] + list(state)
    is_last = last == SLOTS
    return pl.pallas_call(
        functools.partial(sums_kernel, first, last, len(old) + len(new), len(old)),
        out_shape=(
            jax.ShapeDtypeStruct((SLOTS + 8, B), jnp.float32),
            pltpu.HBM(((last - first) * B, E), jnp.bfloat16),
        )
        + ((jax.ShapeDtypeStruct((dp_count, 1, 128), jnp.float32),) if is_last else ()),
        in_specs=[VMEM] * len(operands),
        out_specs=(VMEM, HBM) + ((VMEM,) if is_last else ()),
        scratch_shapes=[pltpu.SemaphoreType.DMA((len(new),))],
        compiler_params=pltpu.CompilerParams(vmem_limit_bytes=12 * MIB),
        cost_estimate=pl.CostEstimate(
            flops=pairs * 2 * B * B * E, bytes_accessed=last * B * E * 2, transcendentals=pairs * B * B
        ),
    )(*operands)


def grad_kernel(*refs):
    unit_refs = refs[: len(STAGES)]
    place_ref, totals_ref, emb_ref, grad_ref, units, sem = refs[len(STAGES) :]
    copies = []
    for k, (ref, row) in enumerate(split_blocks(unit_refs)):
        target = units.at[pl.ds(k * B, B), :]
        copies.append(pltpu.make_async_copy(ref.at[pl.ds(row, B), :], target, sem.at[k]))
    for copy in copies:
        copy.start()
    inverse = 1.0 / totals_ref[:SLOTS, :]
    row_inv = column(inverse[0:1, :])
    row_inv = jnp.concatenate([row_inv, row_inv], axis=1)
    place = jnp.concatenate([place_ref[...], place_ref[...]], axis=1)
    rows = lax.broadcasted_iota(jnp.int32, (B, B), 0)
    lanes = lax.broadcasted_iota(jnp.int32, (B, B), 1)
    emb = emb_ref[...]
    lengths = jnp.sqrt(jnp.sum(emb * emb, axis=1, keepdims=True) + 1e-06)
    unit = emb / lengths
    unit_grad = None
    for start in range(0, SLOTS * B, CHUNK):
        for copy in copies[start // B : (start + CHUNK) // B]:
            copy.wait()
        cols = units[start : start + CHUNK, :]
        raw = nt_dot(units[0:B, :], cols)
        row_w, col_w = [], []
        for k in range(CHUNK // B):
            b = start // B + k
            e = jnp.exp2(raw[:, k * B : (k + 1) * B] * SCALE)
            if b == 0:
                e = jnp.where(rows == lanes, 0.0, e)
            ind = jnp.where(lanes + b * B == place, 1.0, 0.0)
            row_w.append((e * row_inv - ind).astype(jnp.bfloat16))
            col_w.append((e * inverse[b : b + 1, :] - ind).astype(jnp.bfloat16))
        both = jnp.concatenate(
            [jnp.concatenate(row_w, axis=1), jnp.concatenate(col_w, axis=1)], axis=0
        )
        both = jnp.dot(both, cols, preferred_element_type=jnp.float32)
        part = both[:B] + both[B:]
        unit_grad = part if unit_grad is None else unit_grad + part
    unit_grad = unit_grad * (1.0 / TAU)
    along = jnp.sum(unit * unit_grad, axis=1, keepdims=True)
    grad_ref[...] = (unit_grad - unit * along) / lengths


def grads(units, place, totals, embeddings):
    return pl.pallas_call(
        grad_kernel,
        out_shape=jax.ShapeDtypeStruct((B, E), jnp.float32),
        in_specs=[HBM] * len(units) + [VMEM] * 3,
        out_specs=VMEM,
        scratch_shapes=[
            pltpu.VMEM((SLOTS * B, E), jnp.bfloat16),
            pltpu.SemaphoreType.DMA((SLOTS,)),
        ],
        compiler_params=pltpu.CompilerParams(vmem_limit_bytes=16 * MIB),
        cost_estimate=pl.CostEstimate(
            flops=6 * SLOTS * B * B * E, bytes_accessed=SLOTS * B * E * 2, transcendentals=SLOTS * B * B
        ),
    )(*[pltpu.with_memory_space_constraint(part, pltpu.HBM) for part in units], place, totals, embeddings)


def shift_x(value, step):
    dp_count = lax.axis_size("dp")
    perm = []
    for x in range(X):
        for z in range(Z):
            for k in range(dp_count):
                to_x = (x + (step if k % 2 == 0 else -step)) % X
                perm.append(((x * Z + z) * dp_count + k, (to_x * Z + z) * dp_count + k))
    return lax.ppermute(value, ("group", "dp"), perm)


def loss_groups(dp_count):
    segments = ((3, 3, 0, 0), (0, 0, 3, 3), (1, 1, 2, 2), (2, 2, 1, 1))
    return [
        [(x * Z + lows[k // 2 % 4]) * dp_count + k for k in range(dp_count)]
        for x in range(X)
        for lows in segments
    ]


def swap_z(value, mask):
    perm = [(x * Z + z, x * Z + (z ^ mask)) for x in range(X) for z in range(Z)]
    return lax.ppermute(value, "group", perm)


def stack_kernel(first_ref, second_ref, both_ref):
    both_ref[:B, :] = first_ref[...]
    both_ref[B:, :] = second_ref[...]


def stack(first, second):
    return pl.pallas_call(
        stack_kernel,
        out_shape=jax.ShapeDtypeStruct((2 * B, E), jnp.bfloat16),
        in_specs=[VMEM, VMEM],
        out_specs=VMEM,
        compiler_params=pltpu.CompilerParams(vmem_limit_bytes=4 * MIB),
    )(first, second)


def on_device(embeddings, partner):
    dp_count = lax.axis_size("dp")
    group_count = lax.axis_size("group")
    packed = pack(embeddings)
    place, own_place = places(partner, dp_count)

    z1 = swap_z(packed, 1)
    z2 = swap_z(packed, 2)
    near = stack(packed, z1)
    near_1, near_3 = shift_x(near, 1), shift_x(near, 3)
    z3 = swap_z(z2, 1)
    z2_1, z2_3 = shift_x(z2, 1), shift_x(z2, 3)
    z3_1, z3_3 = shift_x(z3, 1), shift_x(z3, 3)

    old, units, state = [], [], ()

    def add(*new):
        first, last = sum(STAGES[len(units) - 1 : len(units)]), STAGES[len(units)]
        part_sums, part_units, *rest = sums(first, last, old, new, place, state, dp_count)
        units.append(part_units)
        old.extend(new)
        return (part_sums,), rest

    near_1, near_3, z2_1 = lax.optimization_barrier((near_1, near_3, z2_1))
    near_2 = shift_x(near_1, 1)
    far_pair = stack(z2_3, z3_3)
    far_pair, near = lax.optimization_barrier((far_pair, near))
    far_2 = shift_x(far_pair, 3)
    state, _ = add(near, z2, z3)
    state, _ = add(near_1, near_3)
    state, _ = add(z2_1, z3_1, z2_3, z3_3)
    state, _ = add(near_2)
    (totals,), (part,) = add(far_2)
    losses = lax.all_to_all(part, ("group", "dp"), 0, 0, axis_index_groups=loss_groups(dp_count))
    gradient = grads(units, own_place, totals, embeddings)
    loss = jnp.sum(losses) / (B * dp_count * group_count)
    return (gradient, loss)


def solution(mesh):
    placed = (P(("group", "dp"), None), P())
    return jax.shard_map(
        on_device,
        mesh=mesh,
        in_specs=placed,
        out_specs=(P(("group", "dp"), None), P()),
        check_vma=False,
    )
```
